32 devices in a mesh: groups: 2 (over y), ctx: 4 (over z), head: 4 (over x, core).
Axes of the slice: x: 2, y: 2, z: 4, core: 2. Of those that a mesh axis runs over, the one named last changes fastest.
Arguments:
- queries: bfloat16 [64, 2048, 128], P(('groups', 'head'), 'ctx'), parts along dimension 0, may hold values from -48 to 48
- key_rows: bfloat16 [8, 2048, 128], P(('groups', 'head'), 'ctx'), parts along dimension 0, may hold values from -6 to 6
- value_rows: bfloat16 [8, 2048, 128], P(('groups', 'head'), 'ctx'), parts along dimension 0, may hold values from -6 to 6
- out_grad: bfloat16 [64, 2048, 128], P(('groups', 'head'), 'ctx'), parts along dimension 0, may hold values from -6 to 6
- link_mask: int32 [32, 11], P(('groups', 'ctx')), parts along dimension 0, may hold values from 0 to 1, as said below
Outputs:
- output: bfloat16 [64, 2048, 128], P(('groups', 'head'), 'ctx'), parts along dimension 0
- query_grad: bfloat16 [64, 2048, 128], P(('groups', 'head'), 'ctx'), parts along dimension 0
- key_grad: bfloat16 [8, 2048, 128], P(('groups', 'head'), 'ctx'), parts along dimension 0
- value_grad: bfloat16 [8, 2048, 128], P(('groups', 'head'), 'ctx'), parts along dimension 0
The draws below stay inside these ranges and needn't reach their ends.
There are 2 independent parts, one for each index of `groups`. The reference program is written for one: setup_inputs(seed, part) draws one part's arguments, and reference() takes and returns one part's arrays. A program takes and returns all parts, laid end to end along the dimension named above; each array names one. Nothing has to cross between parts.
Inputs may be any that keep to these rules, and one draw needn't show every extreme that they name: `link_mask`: column 0 is 1 in every row.
All inputs are finite; a program needn't handle non-finite values.
Results may differ from the reference program's by a relative error of at most 0.028.
Values may be sent and summed in bfloat16 or wider, within the bound.
A program may use at most 64 MiB of HBM per device.

```python
import math
import jax
import jax.numpy as jnp
from jax import lax

HEADS = 8
HD = 128
BLK = 128
NOFF = 11
KVG = 4
SEQ = 2048


def drawn_pair(key):
    key_query, key_keys = jax.random.split(key, 2)
    total_heads = KVG * HEADS
    query_draw = jnp.clip(1.5 * jax.random.normal(key_query, (total_heads, SEQ, HD), jnp.float32), -9.0, 9.0)
    key_draw = jnp.clip(jax.random.normal(key_keys, (KVG, SEQ, HD), jnp.float32), -6.0, 6.0)
    return (query_draw, key_draw)


def draw_queries(key, part):
    return drawn_pair(jax.random.fold_in(key, 11))[0].astype(jnp.bfloat16)


def draw_key_rows(key, part):
    return drawn_pair(jax.random.fold_in(key, 11))[1].astype(jnp.bfloat16)


def draw_link_mask(key, part):
    levels = jax.random.randint(jax.random.fold_in(key, 23), (SEQ // BLK, NOFF), 0, 4)
    kept = (levels > 0).astype(jnp.int32)
    return kept.at[:, 0].set(1)


def level_of(own_key, shape, cuts, least, largest):
    def one(position, parts):
        heights = jax.random.uniform(jax.random.fold_in(jax.random.fold_in(own_key, 6), position), (parts,), jnp.float32, least / len(cuts), largest / len(cuts))
        return jnp.repeat(jnp.exp(heights), shape[position] // parts).reshape((-1,) + (1,) * (len(shape) - position - 1))

    loudness = one(*cuts[0])
    for cut in cuts[1:]:
        loudness = loudness * one(*cut)
    return loudness


def noise(stream_key, dims, width, bound, cuts=(), kind=jnp.bfloat16):
    entries = jax.random.normal(stream_key, dims, jnp.float32) * width
    if len(cuts) > 0:
        entries = level_of(stream_key, dims, cuts, -0.22, 0.18) * entries
    return jnp.clip(entries, min=-bound, max=bound).astype(kind)


def setup_inputs(seed: int = 0, part: int = 0) -> dict:
    keys = jax.random.split(jax.random.key(seed), 6)
    part_splits = jax.random.split(jax.random.fold_in(keys[5], part), 6)
    return {
        "queries": draw_queries(jax.random.fold_in(jax.random.fold_in(keys[5], part), 71), part),
        "key_rows": draw_key_rows(jax.random.fold_in(jax.random.fold_in(keys[5], part), 71), part),
        "value_rows": noise(part_splits[2], (KVG, SEQ, HD), 1.0, 6.0, ((0, 4), (1, 4))),
        "out_grad": noise(part_splits[3], (KVG * HEADS, SEQ, HD), 1.0, 6.0, ((0, 4), (1, 4))),
        "link_mask": draw_link_mask(jax.random.fold_in(jax.random.fold_in(keys[5], part), 71), part),
    }


def one_group(queries, key_rows, value_rows, out_grad, link_mask):
    block_total = SEQ // BLK
    inv_root = 1.0 / math.sqrt(HD)
    offsets = jnp.array([0] + [2 ** slot for slot in range(NOFF - 1)], dtype=jnp.int32)
    query_blocks = queries.reshape(HEADS, block_total, BLK, HD)
    grad_blocks = out_grad.reshape(HEADS, block_total, BLK, HD)
    key_blocks = key_rows.reshape(block_total, BLK, HD)
    value_blocks = value_rows.reshape(block_total, BLK, HD)
    causal = jnp.arange(BLK)[None, :] <= jnp.arange(BLK)[:, None]
    is_diagonal = jnp.arange(NOFF) == 0

    def block_step(running, block_id):
        key_acc, value_acc = running
        source = (block_id - offsets).astype(jnp.int32)
        link_live = (source >= 0) & (link_mask[block_id] == 1)
        source = jnp.maximum(source, 0).astype(jnp.int32)
        key_part = key_blocks[source].astype(jnp.float32)
        value_part = value_blocks[source].astype(jnp.float32)
        query_part = lax.dynamic_index_in_dim(query_blocks, block_id, 1, keepdims=False).astype(jnp.float32)
        grad_part = lax.dynamic_index_in_dim(grad_blocks, block_id, 1, keepdims=False).astype(jnp.float32)
        allowed = link_live[None, :, None] & (causal[:, None, :] | (~is_diagonal)[None, :, None])
        scores = jnp.einsum('htd,jud->htju', query_part, key_part) * inv_root
        scores = jnp.where(allowed[None], scores, -jnp.inf)
        row_max = lax.optimization_barrier(jnp.max(scores, axis=(2, 3), keepdims=True))
        log_total = row_max + jnp.log(lax.optimization_barrier(jnp.sum(jnp.exp(scores - row_max), axis=(2, 3), keepdims=True)))
        weights = jnp.exp(scores - log_total)
        weights_low = lax.optimization_barrier(weights.astype(jnp.bfloat16)).astype(jnp.float32)
        output = jnp.einsum('htju,jud->htd', weights_low, value_part).astype(jnp.bfloat16)
        row_dot = lax.optimization_barrier(jnp.sum(grad_part * output.astype(jnp.float32), axis=-1))[:, :, None, None]
        grad_weights = jnp.einsum('htd,jud->htju', grad_part, value_part)
        grad_scores = weights * (grad_weights - row_dot) * inv_root
        grad_scores = lax.optimization_barrier(grad_scores.astype(jnp.bfloat16)).astype(jnp.float32)
        query_grad = jnp.einsum('htju,jud->htd', grad_scores, key_part).astype(jnp.bfloat16)
        key_part_grad = jnp.einsum('htju,htd->jud', grad_scores, query_part)
        value_part_grad = jnp.einsum('htju,htd->jud', weights_low, grad_part)
        key_acc = key_acc.at[source].add(key_part_grad)
        value_acc = value_acc.at[source].add(value_part_grad)
        return ((key_acc, value_acc), (output, query_grad))
    empty = jnp.zeros((block_total, BLK, HD), jnp.float32)
    (key_acc, value_acc), (outputs, query_grads) = lax.scan(block_step, (empty, empty), jnp.arange(block_total, dtype=jnp.int32))
    output = jnp.transpose(outputs, (1, 0, 2, 3)).reshape(HEADS, SEQ, HD)
    query_grad = jnp.transpose(query_grads, (1, 0, 2, 3)).reshape(HEADS, SEQ, HD)
    key_grad = key_acc.reshape(SEQ, HD).astype(jnp.bfloat16)
    value_grad = value_acc.reshape(SEQ, HD).astype(jnp.bfloat16)
    return (output, query_grad, key_grad, value_grad)

def reference(queries, key_rows, value_rows, out_grad, link_mask):
    grouped_q = queries.reshape(KVG, HEADS, SEQ, HD)
    grouped_g = out_grad.reshape(KVG, HEADS, SEQ, HD)

    def run(items):
        return one_group(items[0], items[1], items[2], items[3], link_mask)
    output, query_grad, key_grad, value_grad = lax.map(run, (grouped_q, key_rows, value_rows, grouped_g))
    return (output.reshape(KVG * HEADS, SEQ, HD), query_grad.reshape(KVG * HEADS, SEQ, HD), key_grad, value_grad)
```

```python
import functools
import math

import jax
import jax.numpy as jnp
from jax import lax
from jax.experimental import pallas as pl
from jax.experimental.pallas import tpu as pltpu
from jax.sharding import PartitionSpec as P

BLK = 128
NOFF = 11
MESH = pl.DeviceIdType.MESH
NEG = -1e30
F32 = jnp.float32
BF16 = jnp.bfloat16


def slot_table(block_count, ctx_size):
    entries = []
    for slot_id in range(NOFF):
        offset = 0 if slot_id == 0 else 2 ** (slot_id - 1)
        if offset < block_count:
            entries.append((slot_id, offset, 0))
        elif offset // block_count < ctx_size:
            entries.append((slot_id, offset, offset // block_count))
    return entries


def hop_of(distance):
    return max(distance // 2, 1)


def dot(a, b, dims):
    return lax.dot_general(a, b, (dims, ((), ())), preferred_element_type=F32)


def kernel(
    ctx_size,
    entries,
    distances,
    mask_ref,
    q_ref,
    g_ref,
    k_ref,
    v_ref,
    out_ref,
    dq_ref,
    dk_ref,
    dv_ref,
    own_kv,
    far_kv,
    own_grad,
    pend_grad,
    stage,
    landed,
    w_scr,
    ds_scr,
    kv_send,
    kv_recv,
    g_send,
    g_recv,
):
    me = lax.axis_index("ctx")
    heads, row_count, head_size = q_ref.shape
    block_count = row_count // BLK
    inv_root = 1.0 / math.sqrt(head_size)
    scale = inv_root * math.log2(math.e)
    place = {distance: i for i, distance in enumerate(distances)}

    def rows(block):
        return pl.ds(block * BLK, BLK)

    def kv_copy(distance, block):
        i = place[distance]
        if distance == 1:
            source = own_kv.at[rows(block)]
        else:
            source = far_kv.at[place[distance // 2], rows(block)]
        return pltpu.make_async_remote_copy(
            src_ref=source,
            dst_ref=far_kv.at[i, rows(block)],
            send_sem=kv_send.at[i, block],
            recv_sem=kv_recv.at[i, block],
            device_id={"ctx": me + hop_of(distance)},
            device_id_type=MESH,
        )

    def kv_sends(distance):
        hop = hop_of(distance)
        return (me + hop < ctx_size) & (me >= distance - hop) if distance > 1 else me + hop < ctx_size

    def grad_copy(distance, block):
        i = place[distance]
        return pltpu.make_async_remote_copy(
            src_ref=stage.at[i, rows(block)],
            dst_ref=landed.at[i, rows(block)],
            send_sem=g_send.at[i, block],
            recv_sem=g_recv.at[i, block],
            device_id={"ctx": me - hop_of(distance)},
            device_id_type=MESH,
        )

    def grad_arrives(distance):
        hop = hop_of(distance)
        return (me + hop < ctx_size) & (me + hop >= distance)

    own_kv[:, :head_size] = k_ref[0]
    own_kv[:, head_size:] = v_ref[0]
    for distance in distances:

        @pl.when(me < distance)
        def _(distance=distance):
            far_kv[place[distance]] = jnp.zeros(far_kv.shape[1:], BF16)

    hops = sorted(set(hop_of(distance) for distance in distances))
    barrier = pltpu.get_barrier_semaphore()
    for hop in hops:

        @pl.when(me + hop < ctx_size)
        def _(hop=hop):
            pl.semaphore_signal(barrier, inc=1, device_id={"ctx": me + hop}, device_id_type=MESH)

        @pl.when(me >= hop)
        def _(hop=hop):
            pl.semaphore_signal(barrier, inc=1, device_id={"ctx": me - hop}, device_id_type=MESH)

    peers = 0
    for hop in hops:
        peers = peers + (me + hop < ctx_size).astype(jnp.int32) + (me >= hop).astype(jnp.int32)
    pl.semaphore_wait(barrier, peers)

    first_order = [0] + list(range(block_count - 1, 0, -1))

    @pl.when(kv_sends(1))
    def _():
        for block in first_order:
            kv_copy(1, block).start()

    def receive(distance):
        for block in range(block_count):

            @pl.when(me >= distance)
            def _(block=block):
                kv_copy(distance, block).wait_recv()

            if 2 * distance in place:

                @pl.when(kv_sends(2 * distance))
                def _(block=block):
                    kv_copy(2 * distance, block).start()

    for distance in distances[:-1]:
        receive(distance)

    own_set = set()
    pend_set = set()

    def add_own(block, value_k, value_v):
        for part, value in ((slice(0, head_size), value_k), (slice(head_size, None), value_v)):
            if block in own_set:
                own_grad[rows(block), part] += value
            else:
                own_grad[rows(block), part] = value
        own_set.add(block)

    def add_pend(distance, block, value_k, value_v):
        i = place[distance]
        for part, value in ((slice(0, head_size), value_k), (slice(head_size, None), value_v)):
            if (i, block) in pend_set:
                pend_grad[i, rows(block), part] += value
            else:
                pend_grad[i, rows(block), part] = value
        pend_set.add((i, block))

    head_step = 2 if heads % 2 == 0 else 1
    step_rows = head_step * BLK

    def piece(block, offset, distance, part):
        if distance > 0:
            return far_kv[place[distance], rows(block), part]
        if block >= offset:
            return own_kv[rows(block - offset), part]
        return far_kv[place[1], rows(block - offset + block_count), part]

    def compute(block):
        keys = jnp.concatenate(
            [piece(block, offset, distance, slice(0, head_size)) for _, offset, distance in entries],
            axis=0,
        )
        values = jnp.concatenate(
            [
                piece(block, offset, distance, slice(head_size, None))
                for _, offset, distance in entries
            ],
            axis=0,
        )
        block_id = me * block_count + block
        row_ids = lax.broadcasted_iota(jnp.int32, (step_rows, BLK), 0) % BLK
        causal = lax.broadcasted_iota(jnp.int32, (step_rows, BLK), 1) <= row_ids
        bias = []
        for slot_id, offset, _ in entries:
            live = (mask_ref[block, slot_id] == 1) & (block_id >= offset)
            bias.append(jnp.where(live, 0.0, NEG).astype(F32))
        for step in range(heads // head_step):
            part = (slice(step * head_step, (step + 1) * head_step), rows(block))
            q = q_ref[part].reshape(step_rows, head_size)
            g = g_ref[part].reshape(step_rows, head_size)
            s = dot(q, keys, ((1,), (1,)))
            pieces = []
            top = None
            for position, (slot_id, offset, _) in enumerate(entries):
                t = s[:, position * BLK : (position + 1) * BLK]
                if offset == 0:
                    t = jnp.where(causal, t, NEG)
                else:
                    t = t + bias[position]
                pieces.append(t)
                top = t if top is None else jnp.maximum(top, t)
            top = jnp.max(top, axis=1, keepdims=True) * scale
            p = jnp.exp2(jnp.concatenate(pieces, axis=1) * scale - top)
            total = jnp.sum(p, axis=1, keepdims=True)
            w = p * (1.0 / total)
            w_low = w.astype(BF16)
            out = dot(w_low, values, ((1,), (0,))).astype(BF16)
            row_dot = jnp.sum(g.astype(F32) * out.astype(F32), axis=1, keepdims=True)
            gw = dot(g, values, ((1,), (1,)))
            ds = (w * (gw - row_dot)).astype(BF16)
            dq = dot(ds, keys, ((1,), (0,))) * inv_root
            out_ref[part] = out.reshape(head_step, BLK, head_size)
            dq_ref[part] = dq.astype(BF16).reshape(head_step, BLK, head_size)
            w_scr[step * step_rows : (step + 1) * step_rows] = w_low
            ds_scr[step * step_rows : (step + 1) * step_rows] = ds
        q_all = q_ref[:, rows(block)].reshape(heads * BLK, head_size)
        g_all = g_ref[:, rows(block)].reshape(heads * BLK, head_size)
        dk = dot(ds_scr[...], q_all, ((0,), (0,))) * inv_root
        dv = dot(w_scr[...], g_all, ((0,), (0,)))
        for position, (_, offset, distance) in enumerate(entries):
            dk_part = dk[position * BLK : (position + 1) * BLK]
            dv_part = dv[position * BLK : (position + 1) * BLK]
            if distance > 0:
                add_pend(distance, block, dk_part, dv_part)
            elif block >= offset:
                add_own(block - offset, dk_part, dv_part)
            else:
                add_pend(1, block - offset + block_count, dk_part, dv_part)

    def forward_grad(distance, block):
        i = place[distance]
        if 2 * distance in place:
            arrives = grad_arrives(2 * distance)

            @pl.when(arrives)
            def _():
                grad_copy(2 * distance, block).wait_recv()
                total = pend_grad[i, rows(block)] + landed[place[2 * distance], rows(block)].astype(F32)
                stage[i, rows(block)] = total.astype(BF16)

            @pl.when(jnp.logical_not(arrives))
            def _():
                stage[i, rows(block)] = pend_grad[i, rows(block)].astype(BF16)
        else:
            stage[i, rows(block)] = pend_grad[i, rows(block)].astype(BF16)

        @pl.when(me >= distance)
        def _():
            grad_copy(distance, block).start()

    def drain(block):
        for distance in reversed(distances[:-1]):
            forward_grad(distance, block)

    def finish(block):
        @pl.when(grad_arrives(1))
        def _():
            grad_copy(1, block).wait_recv()
            own_grad[rows(block)] += landed[place[1], rows(block)].astype(F32)

        dk_ref[0, rows(block)] = own_grad[rows(block), :head_size].astype(BF16)
        dv_ref[0, rows(block)] = own_grad[rows(block), head_size:].astype(BF16)

    last = distances[-1]
    for block in range(block_count):

        @pl.when(me >= last)
        def _(block=block):
            kv_copy(last, block).wait_recv()

        compute(block)
        forward_grad(last, block)
        if block >= 1:
            drain(block - 1)
    drain(block_count - 1)
    for block in range(block_count):
        finish(block)

    for distance in distances:

        @pl.when(kv_sends(distance))
        def _(distance=distance):
            for block in range(block_count):
                kv_copy(distance, block).wait_send()

        @pl.when(me >= distance)
        def _(distance=distance):
            for block in range(block_count):
                grad_copy(distance, block).wait_send()


def local(queries, key_rows, value_rows, out_grad, link_mask):
    heads, row_count, head_size = queries.shape
    block_count = row_count // BLK
    ctx_size = lax.axis_size("ctx")
    entries = slot_table(block_count, ctx_size)
    distances = sorted(set(entry[2] for entry in entries if entry[2] > 0))
    levels = len(distances)
    keys_wide = len(entries) * BLK
    vmem = pl.BlockSpec(memory_space=pltpu.VMEM)
    flops = 10 * heads * row_count * keys_wide * head_size
    return pl.pallas_call(
        functools.partial(kernel, ctx_size, entries, distances),
        out_shape=(
            jax.ShapeDtypeStruct(queries.shape, BF16),
            jax.ShapeDtypeStruct(queries.shape, BF16),
            jax.ShapeDtypeStruct(key_rows.shape, BF16),
            jax.ShapeDtypeStruct(value_rows.shape, BF16),
        ),
        in_specs=[pl.BlockSpec(memory_space=pltpu.SMEM), vmem, vmem, vmem, vmem],
        out_specs=(vmem, vmem, vmem, vmem),
        scratch_shapes=[
            pltpu.VMEM((row_count, 2 * head_size), BF16),
            pltpu.VMEM((levels, row_count, 2 * head_size), BF16),
            pltpu.VMEM((row_count, 2 * head_size), F32),
            pltpu.VMEM((levels, row_count, 2 * head_size), F32),
            pltpu.VMEM((levels, row_count, 2 * head_size), BF16),
            pltpu.VMEM((levels, row_count, 2 * head_size), BF16),
            pltpu.VMEM((heads * BLK, keys_wide), BF16),
            pltpu.VMEM((heads * BLK, keys_wide), BF16),
            pltpu.SemaphoreType.DMA((levels, block_count)),
            pltpu.SemaphoreType.DMA((levels, block_count)),
            pltpu.SemaphoreType.DMA((levels, block_count)),
            pltpu.SemaphoreType.DMA((levels, block_count)),
        ],
        compiler_params=pltpu.CompilerParams(
            collective_id=0, has_side_effects=True, vmem_limit_bytes=56 * 1024 * 1024
        ),
        cost_estimate=pl.CostEstimate(
            flops=flops,
            bytes_accessed=8 * heads * row_count * head_size,
            transcendentals=heads * row_count * keys_wide,
        ),
    )(link_mask, queries, out_grad, key_rows, value_rows)


def solution(mesh):
    return jax.shard_map(
        local,
        mesh=mesh,
        in_specs=(
            P(("groups", "head"), "ctx", None),
            P(("groups", "head"), "ctx", None),
            P(("groups", "head"), "ctx", None),
            P(("groups", "head"), "ctx", None),
            P(("groups", "ctx"), None),
        ),
        out_specs=(
            P(("groups", "head"), "ctx", None),
            P(("groups", "head"), "ctx", None),
            P(("groups", "head"), "ctx", None),
            P(("groups", "head"), "ctx", None),
        ),
        check_vma=False,
    )
```
